512 devices in a mesh: row: 16 (over z_lo, x), col: 32 (over y, z_hi, core).
Axes of the slice: x: 4, y: 4, z: 16 (z_hi: 4, z_lo: 4; z = z_hi * 4 + z_lo), core: 2. Of those that a mesh axis runs over, the one named last changes fastest.
Arguments:
- x_cols: bfloat16 [8, 262144], P(None, ('col', 'row')), may hold values from -6 to 6
- diag_rows: float32 [262144], P(('row', 'col')), may hold values from 0.5 to 2
- theta: float32 [8], replicated, may hold values from -1 to 1
- tiles: bfloat16 [16, 32, 96, 128, 128], P('row', 'col'), may hold values from -0.109375 to 0.109375
- tile_rows: int32 [16, 32, 96], P('row', 'col'), may hold values from 0 to 127, as said below
- tile_cols: int32 [16, 32, 96], P('row', 'col'), may hold values from 0 to 63, as said below
- counts: int32 [16, 32], P('row', 'col'), may hold values from 48 to 96, as said below
Outputs:
- resid: float32 [8, 262144], P(None, ('row', 'col'))
- image: float32 [8, 262144], P(None, ('col', 'row'))
The draws below stay inside these ranges and needn't reach their ends.
Inputs may be any that keep to these rules, and one draw needn't show every extreme that they name: Within one device block, the pairs (tile_rows, tile_cols) of its 96 slots are all different. `tile_cols`: paired with tile_rows slot by slot. `counts`: slots at or past a block's count are unused and their tiles hold arbitrary values. Some block has all 96 slots in use.
All inputs are finite; a program needn't handle non-finite values.
Results may differ from the reference program's by a relative error of at most 0.0023.
Values may be sent and summed in bfloat16 or wider, within the bound.
No kernel may reach another device: no remote copies, remote signals or barrier semaphores. Data moves between devices by JAX's collectives and lax.ppermute only.
A program may use at most 64 MiB of HBM per device.

```python
import math
import jax
import jax.numpy as jnp
from jax import lax

NVEC = 8
TILE = 128
SHARE = 512
SLOTS = 96
BASIS = 262144
TROWS = 128
TCOLS = 64
N_ROW = 16
N_COL = 32


def tile_positions(key):
    inner = jax.random.fold_in(key, 7)
    keys = jax.random.split(inner, N_ROW * N_COL)

    def choose(single):
        return jax.random.permutation(single, TROWS * TCOLS)[:SLOTS]
    return jax.vmap(choose)(keys).reshape(N_ROW, N_COL, SLOTS).astype(jnp.int32)


def draw_tile_rows(key, part):
    return (tile_positions(key) // TCOLS).astype(jnp.int32)


def draw_tile_cols(key, part):
    return (tile_positions(key) % TCOLS).astype(jnp.int32)


def draw_counts(key, part):
    first = jax.random.fold_in(key, 11)
    second = jax.random.fold_in(key, 13)
    base = jax.random.randint(first, (N_ROW * N_COL,), SLOTS // 2, SLOTS + 1, dtype=jnp.int32)
    chosen = jax.random.randint(second, (), 0, N_ROW * N_COL, dtype=jnp.int32)
    places = jnp.arange(N_ROW * N_COL, dtype=jnp.int32)
    filled = jnp.where(places == chosen, SLOTS, base)
    return filled.reshape(N_ROW, N_COL).astype(jnp.int32)


def level_of(own_key, shape, cuts, smallest, largest):
    level, own = 1.0, jax.random.fold_in(own_key, 6)
    for axis_at, shards_of in cuts:
        draws = jnp.exp(jax.random.uniform(jax.random.fold_in(own, axis_at), (shards_of,), jnp.float32, smallest / len(cuts), largest / len(cuts)))
        level = level * jnp.repeat(draws, shape[axis_at] // shards_of).reshape([-1 if axis == axis_at else 1 for axis in range(len(shape))])
    return level


def gaussian(rng, shape, width, bound, pieces=(), kind=jnp.bfloat16):
    result = width * jax.random.normal(rng, shape, jnp.float32)
    if pieces:
        result = result * level_of(rng, shape, pieces, -0.22, 0.18)
    return jnp.clip(result, -bound, bound).astype(kind)


def setup_inputs(seed: int = 0) -> dict:
    arg_keys = jax.random.split(jax.random.key(seed), 8)
    x_cols = gaussian(arg_keys[0], (NVEC, BASIS), 1.0, 6.0, ((1, 512),))
    diag_rows = jnp.clip(jnp.exp(math.log(2.0) - 1.3862944 * jax.random.uniform(arg_keys[1], (BASIS,), jnp.float32) ** level_of(arg_keys[1], (BASIS,), ((0, 512),), -0.2, 0.2)), 0.5, 2.0)
    theta = jnp.clip(jax.random.uniform(arg_keys[2], (NVEC,), jnp.float32, -1.0, 1.0), -1.0, 1.0)
    tiles = gaussian(arg_keys[3], (N_ROW, N_COL, SLOTS, TILE, TILE), (16384 * SLOTS // SHARE) ** -0.5, 0.109375, ((0, 16), (1, 32)))
    tile_rows = draw_tile_rows(jax.random.fold_in(arg_keys[7], 71), 0)
    tile_cols = draw_tile_cols(jax.random.fold_in(arg_keys[7], 71), 0)
    counts = draw_counts(jax.random.fold_in(arg_keys[7], 71), 0)
    return dict(x_cols=x_cols, diag_rows=diag_rows, theta=theta, tiles=tiles, tile_rows=tile_rows, tile_cols=tile_cols, counts=counts)


def spread(vectors):
    return vectors.reshape(NVEC, -1, TILE).transpose(1, 0, 2)


def gather_back(blocks):
    return blocks.transpose(1, 0, 2).reshape(NVEC, -1)


def reference(x_cols, diag_rows, theta, tiles, tile_rows, tile_cols, counts):
    slot_ids = jnp.arange(SLOTS, dtype=jnp.int32)
    vectors_in = spread(x_cols)
    devices = jnp.arange(N_ROW * N_COL, dtype=jnp.int32)

    def forward(totals, device):
        row_index = device // N_COL
        col_index = device % N_COL
        block_tiles = tiles[row_index, col_index].astype(jnp.float32)
        in_use = slot_ids < counts[row_index, col_index]
        columns = lax.dynamic_slice_in_dim(vectors_in, (col_index * TCOLS).astype(jnp.int32), TCOLS, 0)
        picked = jnp.take(columns, tile_cols[row_index, col_index], axis=0).astype(jnp.float32)
        products = jnp.einsum('kab,knb->kna', block_tiles, picked)
        products = jnp.where(in_use[:, None, None], products, 0.0)
        summed = jax.ops.segment_sum(products, tile_rows[row_index, col_index], num_segments=TROWS)
        start = (row_index * TROWS).astype(jnp.int32)
        current = lax.dynamic_slice_in_dim(totals, start, TROWS, 0)
        return lax.dynamic_update_slice_in_dim(totals, current + summed, start, 0), None

    empty = jnp.zeros((BASIS // TILE, NVEC, TILE), jnp.float32)
    applied, unused = lax.scan(forward, empty, devices)
    resid_blocks = applied - theta[None, :, None] * vectors_in.astype(jnp.float32)
    scaled = (resid_blocks / diag_rows.reshape(-1, 1, TILE)).astype(jnp.bfloat16)

    def backward(totals, device):
        row_index = device // N_COL
        col_index = device % N_COL
        block_tiles = tiles[row_index, col_index].astype(jnp.float32)
        in_use = slot_ids < counts[row_index, col_index]
        rows = lax.dynamic_slice_in_dim(scaled, (row_index * TROWS).astype(jnp.int32), TROWS, 0)
        picked = jnp.take(rows, tile_rows[row_index, col_index], axis=0).astype(jnp.float32)
        products = jnp.einsum('kab,kna->knb', block_tiles, picked)
        products = jnp.where(in_use[:, None, None], products, 0.0)
        summed = jax.ops.segment_sum(products, tile_cols[row_index, col_index], num_segments=TCOLS)
        start = (col_index * TCOLS).astype(jnp.int32)
        current = lax.dynamic_slice_in_dim(totals, start, TCOLS, 0)
        return lax.dynamic_update_slice_in_dim(totals, current + summed, start, 0), None

    image_blocks, unused_two = lax.scan(backward, empty, devices)
    return gather_back(resid_blocks), gather_back(image_blocks)
```

```python
import functools

import jax
import jax.numpy as jnp
from jax import lax
from jax.experimental import pallas as pl
from jax.experimental.pallas import tpu as pltpu
from jax.sharding import PartitionSpec as P

UNROLL = 8
COL_STEPS = (1, 8, 24, 2, 6)
ROW_STEPS = (1, 3, 4, 8)


def col_place(d):
    b = [(d >> i) & 1 for i in range(5)]
    return b[0] * 16 + (b[3] ^ b[4]) * 8 + b[4] * 4 + (b[1] ^ b[2]) * 2 + b[2]


def row_place(d):
    b = [(d >> i) & 1 for i in range(4)]
    return (b[0] ^ b[1]) * 8 + b[1] * 4 + b[2] * 2 + b[3]


def forward(me_ref, at_ref, from_ref, tiles_ref, x_ref, theta_ref, out_ref, total):
    share = 4
    total[...] = jnp.zeros_like(total)
    row, col = me_ref[0], me_ref[1]

    @pl.when(row == col // 2)
    def _():
        theta = theta_ref[...]
        first = (col % 2) * 16

        def shift(s, carry):
            q = row_place(s ^ row) * share
            p = col_place((first + s) ^ col) * share
            for j in range(share):
                total[p + j] = -theta * x_ref[q + j].astype(jnp.float32)
            return carry

        lax.fori_loop(0, 16, shift, 0)

    def step(i, carry):
        for u in range(UNROLL):
            k = i * UNROLL + u
            part = lax.dot_general(
                x_ref[from_ref[k]],
                tiles_ref[k],
                (((1,), (1,)), ((), ())),
                preferred_element_type=jnp.float32,
            )
            p = at_ref[k]
            total[p] = total[p] + part
        return carry

    lax.fori_loop(0, me_ref[2], step, 0)
    n = out_ref.shape[0]
    out_ref[...] = total[:n]


def backward(me_ref, from_ref, at_ref, tiles_ref, scaled_ref, out_ref, total):
    total[...] = jnp.zeros_like(total)

    def step(i, carry):
        for u in range(UNROLL):
            k = i * UNROLL + u
            part = jnp.dot(
                scaled_ref[from_ref[k]],
                tiles_ref[k],
                preferred_element_type=jnp.float32,
            )
            q = at_ref[k]
            total[q] = total[q] + part
        return carry

    lax.fori_loop(0, me_ref[2], step, 0)
    n = out_ref.shape[0]
    out_ref[...] = total[:n]


def swap(value, axis, step):
    n = lax.axis_size(axis)
    return lax.ppermute(value, axis, [(i, i ^ step) for i in range(n)])


def gather(own, axis, steps):
    for step in reversed(steps):
        own = jnp.concatenate([own, swap(own, axis, step)], axis=0)
    return own


def scatter_sum(parts, axis, steps):
    for step in steps:
        half = parts.shape[0] // 2
        parts = parts[:half] + swap(parts[half:], axis, step)
    return parts


def blocks_of(vectors):
    return vectors.reshape(vectors.shape[0], -1, 128).transpose(1, 0, 2)


def vectors_of(blocks):
    return blocks.transpose(1, 0, 2).reshape(blocks.shape[1], -1)


def body(x_cols, diag_rows, theta, tiles, tile_rows, tile_cols, counts):
    row, col = lax.axis_index("row"), lax.axis_index("col")
    tiles = tiles[0, 0]
    rows, cols, count = tile_rows[0, 0], tile_cols[0, 0], counts[0, 0]
    slots, width = tiles.shape[0], tiles.shape[1]
    used = jnp.arange(slots, dtype=jnp.int32) < count
    row_at = col_place((rows // 4) ^ col) * 4 + rows % 4
    col_at = row_place((cols // 4) ^ row) * 4 + cols % 4
    row_sum_at = jnp.where(used, row_at, 128)
    col_sum_at = jnp.where(used, col_at, 64)
    me = jnp.stack([row, col, (count + UNROLL - 1) // UNROLL]).astype(jnp.int32)
    smem = pl.BlockSpec(memory_space=pltpu.SMEM)
    vmem = pl.BlockSpec(memory_space=pltpu.VMEM)
    params = pltpu.CompilerParams(vmem_limit_bytes=24 * 1024 * 1024)
    cost = pl.CostEstimate(flops=2 * slots * 8 * width * width, bytes_accessed=4 << 20, transcendentals=0)

    x_all = gather(blocks_of(x_cols), "row", ROW_STEPS)
    partial = pl.pallas_call(
        forward,
        out_shape=jax.ShapeDtypeStruct((128, 8, width), jnp.float32),
        in_specs=[smem, smem, smem, vmem, vmem, vmem],
        out_specs=vmem,
        scratch_shapes=[pltpu.VMEM((136, 8, width), jnp.float32)],
        compiler_params=params,
        cost_estimate=cost,
    )(me, row_sum_at, col_at, tiles, x_all, jnp.broadcast_to(theta[:, None], (8, width)))
    resid = scatter_sum(partial, "col", COL_STEPS)
    scaled = (resid / diag_rows.reshape(-1, 1, width)).astype(jnp.bfloat16)
    scaled_all = gather(scaled, "col", COL_STEPS)
    back = pl.pallas_call(
        backward,
        out_shape=jax.ShapeDtypeStruct((64, 8, width), jnp.float32),
        in_specs=[smem, smem, smem, vmem, vmem],
        out_specs=vmem,
        scratch_shapes=[pltpu.VMEM((72, 8, width), jnp.float32)],
        compiler_params=params,
        cost_estimate=cost,
    )(me, row_at, col_sum_at, tiles, scaled_all)
    image = scatter_sum(back, "row", ROW_STEPS)
    return vectors_of(resid), vectors_of(image)


def solution(mesh):
    return jax.shard_map(
        body,
        mesh=mesh,
        in_specs=(
            P(None, ("col", "row")),
            P(("row", "col")),
            P(),
            P("row", "col", None, None, None),
            P("row", "col", None),
            P("row", "col", None),
            P("row", "col"),
        ),
        out_specs=(P(None, ("row", "col")), P(None, ("col", "row"))),
        check_vma=False,
    )
```

```python
import functools

import jax
import jax.numpy as jnp
from jax import lax
from jax.experimental import pallas as pl
from jax.experimental.pallas import tpu as pltpu
from jax.sharding import Mesh, PartitionSpec as P

ROW = ("zl", "x")
COL = ("y", "zh", "c")
AT_ROW, AT_COL, AT_CORE = 96, 97, 98


def place(share, core):
    y, zh, c = share >> 3, (share >> 1) & 3, share & 1
    return ((c ^ core) << 4) | (y << 2) | zh


def prepare(tiles_ref, theta_ref, diag_ref, lines_ref, block_ref):
    line = lax.broadcasted_iota(jnp.int32, lines_ref.shape, 0)
    lines = jnp.zeros(lines_ref.shape, jnp.float32)
    for n in range(8):
        lines = jnp.where(line == n, theta_ref[n], lines)
    lines_ref[...] = lines
    block_ref[0, :4] = diag_ref[...]
    block_ref[0, 4:] = jnp.zeros((4, 128), jnp.float32)


def forward(table_ref, tiles_ref, lines_ref, x_ref, out_ref, total):
    total[...] = jnp.zeros_like(total)
    row, col = table_ref[AT_ROW], table_ref[AT_COL]

    @pl.when(row == col >> 1)
    def _():
        first = (col & 1) * 16

        def shift(s, carry):
            p = place(first + s, table_ref[AT_CORE]) * 4
            for j in range(4):
                total[p + j] = -lines_ref[...] * x_ref[s * 4 + j].astype(jnp.float32)
            return carry

        lax.fori_loop(0, 16, shift, 0)

    for i in range(48):
        v, w = table_ref[2 * i], table_ref[2 * i + 1]
        both = jnp.concatenate([x_ref[v & 63], x_ref[w & 63]], axis=0)
        part = lax.dot_general(
            both, tiles_ref[i], (((1,), (1,)), ((), ())), preferred_element_type=jnp.float32
        )
        total[v >> 8] = total[v >> 8] + part[:8, :128]
        total[w >> 8] = total[w >> 8] + part[8:, 128:]
    out_ref[...] = total[:128]


def backward(table_ref, tiles_ref, scaled_ref, out_ref, total):
    total[...] = jnp.zeros_like(total)
    for i in range(48):
        v, w = table_ref[2 * i], table_ref[2 * i + 1]
        a, b = scaled_ref[(v >> 8) & 127], scaled_ref[(w >> 8) & 127]
        none = jnp.zeros_like(a)
        both = jnp.concatenate(
            [jnp.concatenate([a, none], axis=0), jnp.concatenate([none, b], axis=0)], axis=1
        )
        part = jnp.dot(both, tiles_ref[i], preferred_element_type=jnp.float32)
        total[v & 255] = total[v & 255] + part[:8]
        total[w & 255] = total[w & 255] + part[8:]
    out_ref[...] = total[:64].astype(out_ref.dtype)


def swap_cores(value):
    return lax.ppermute(value, "c", [(0, 1), (1, 0)])


def to_all(own, axes):
    copies = jnp.broadcast_to(own[None], (lax.axis_size(axes), *own.shape))
    return lax.all_to_all(copies, axes, 0, 0)


def sum_shares(parts, axes):
    n = lax.axis_size(axes)
    parts = parts.reshape(n, parts.shape[0] // n, *parts.shape[1:])
    return jnp.sum(lax.all_to_all(parts, axes, 0, 0).astype(jnp.float32), axis=0)


def vectors_of(blocks):
    return blocks.transpose(1, 0, 2).reshape(blocks.shape[1], -1)


def body(x_cols, diag_rows, theta, tiles, tile_rows, tile_cols, counts):
    core = lax.axis_index("c")
    slots, width = tiles.shape[2], tiles.shape[3]
    rows = jnp.pad(tile_rows[0, 0], (0, 32))
    cols = jnp.pad(tile_cols[0, 0], (0, 32))
    slot = jnp.arange(slots + 32, dtype=jnp.int32)
    used = slot < counts[0, 0]
    table = jnp.where(used, ((place(rows >> 2, core) << 2) | (rows & 3)) << 8 | cols, 128 << 8 | 64)
    table = jnp.where(slot == AT_ROW, lax.axis_index(ROW), table)
    table = jnp.where(slot == AT_COL, lax.axis_index(COL), table)
    table = jnp.where(slot == AT_CORE, core, table).astype(jnp.int32)

    smem = pl.BlockSpec(memory_space=pltpu.SMEM)
    vmem = pl.BlockSpec(memory_space=pltpu.VMEM)
    params = pltpu.CompilerParams(vmem_limit_bytes=16 * 1024 * 1024)
    cost = pl.CostEstimate(flops=2 * slots * 8 * width * width, bytes_accessed=4 << 20, transcendentals=0)
    f32 = functools.partial(jax.ShapeDtypeStruct, dtype=jnp.float32)

    tiles_here = tiles.reshape(slots // 2, 2 * width, width)
    lines, diag_block = pl.pallas_call(
        prepare,
        out_shape=(f32((8, width)), f32((1, 8, width))),
        in_specs=[vmem, smem, vmem],
        out_specs=(vmem, vmem),
        compiler_params=params,
        cost_estimate=cost,
    )(tiles_here, theta, diag_rows.reshape(4, width))

    own = x_cols.reshape(8, 4, width).transpose(1, 0, 2)
    x_all = to_all(own, ROW).reshape(64, 8, width)
    partial = pl.pallas_call(
        forward,
        out_shape=f32((128, 8, width)),
        in_specs=[smem, vmem, vmem, vmem],
        out_specs=vmem,
        scratch_shapes=[pltpu.VMEM((136, 8, width), jnp.float32)],
        compiler_params=params,
        cost_estimate=cost,
    )(table, tiles_here, lines, x_all)

    partial = sum_shares(partial[:64] + swap_cores(partial[64:]), "y")
    got = to_all(jnp.concatenate([partial, diag_block], axis=0), "zh")
    resid = jnp.sum(got[:, :16], axis=0)
    diag = got[:, 16, :4].reshape(16, 1, width)
    scaled = to_all((resid / diag).astype(jnp.bfloat16), "y").reshape(64, 8, width)
    scaled = jnp.concatenate([scaled, swap_cores(scaled)], axis=0)

    back = pl.pallas_call(
        backward,
        out_shape=f32((64, 8, width)),
        in_specs=[smem, vmem, vmem],
        out_specs=vmem,
        scratch_shapes=[pltpu.VMEM((72, 8, width), jnp.float32)],
        compiler_params=params,
        cost_estimate=cost,
    )(table, tiles_here, scaled)
    image = sum_shares(back, ROW)
    resid = lax.dynamic_slice_in_dim(resid, lax.axis_index("zh") * 4, 4, 0)
    return vectors_of(resid), vectors_of(image)


def solution(mesh):
    fine = Mesh(mesh.devices.reshape(4, 4, 4, 4, 2), ROW + COL)
    return jax.shard_map(
        body,
        mesh=fine,
        in_specs=(
            P(None, COL + ROW),
            P(ROW + COL),
            P(),
            P(ROW, COL, None, None, None),
            P(ROW, COL, None),
            P(ROW, COL, None),
            P(ROW, COL),
        ),
        out_specs=(P(None, ROW + COL), P(None, COL + ROW)),
        check_vma=False,
    )
```

```python
import functools

import jax
import jax.numpy as jnp
from jax import lax
from jax.experimental import pallas as pl
from jax.experimental.pallas import tpu as pltpu
from jax.sharding import Mesh, PartitionSpec as P

ROW = ("zl", "x")
COL = ("y", "zh", "c")
AT_ROW, AT_COL, AT_CORE = 96, 97, 98


def place(share, core):
    y, zh, c = share >> 3, (share >> 1) & 3, share & 1
    return ((c ^ core) << 4) | (y << 2) | zh


def prepare(theta_ref, lines_ref):
    line = lax.broadcasted_iota(jnp.int32, lines_ref.shape, 0)
    lines = jnp.zeros(lines_ref.shape, jnp.float32)
    for n in range(8):
        lines = jnp.where(line == n, theta_ref[n], lines)
    lines_ref[...] = lines


def forward(table_ref, tiles_ref, lines_ref, x_ref, out_ref, total):
    total[...] = jnp.zeros_like(total)
    row, col = table_ref[AT_ROW], table_ref[AT_COL]

    @pl.when(row == col >> 1)
    def _():
        first = (col & 1) * 16

        def shift(s, carry):
            p = place(first + s, table_ref[AT_CORE]) * 4
            for j in range(4):
                total[p + j] = -lines_ref[...] * x_ref[s * 4 + j].astype(jnp.float32)
            return carry

        lax.fori_loop(0, 16, shift, 0)

    for i in range(48):
        v, w = table_ref[2 * i], table_ref[2 * i + 1]
        both = jnp.concatenate([x_ref[v & 63], x_ref[w & 63]], axis=0)
        part = lax.dot_general(
            both, tiles_ref[i], (((1,), (1,)), ((), ())), preferred_element_type=jnp.float32
        )
        total[v >> 8] = total[v >> 8] + part[:8, :128]
        total[w >> 8] = total[w >> 8] + part[8:, 128:]
    out_ref[...] = total[:128]


def backward(table_ref, tiles_ref, scaled_ref, out_ref, total):
    total[...] = jnp.zeros_like(total)
    half = table_ref[AT_CORE] << 6
    for i in range(48):
        v, w = table_ref[2 * i], table_ref[2 * i + 1]
        a, b = scaled_ref[((v >> 8) & 127) ^ half], scaled_ref[((w >> 8) & 127) ^ half]
        none = jnp.zeros_like(a)
        both = jnp.concatenate(
            [jnp.concatenate([a, none], axis=0), jnp.concatenate([none, b], axis=0)], axis=1
        )
        part = jnp.dot(both, tiles_ref[i], preferred_element_type=jnp.float32)
        total[v & 255] = total[v & 255] + part[:8]
        total[w & 255] = total[w & 255] + part[8:]
    out_ref[...] = total[:64].astype(out_ref.dtype)


def to_all(own, axes):
    copies = jnp.broadcast_to(own[None], (lax.axis_size(axes), *own.shape))
    return lax.all_to_all(copies, axes, 0, 0)


def sum_shares(parts, axes):
    n = lax.axis_size(axes)
    parts = parts.reshape(n, parts.shape[0] // n, *parts.shape[1:])
    return jnp.sum(lax.all_to_all(parts, axes, 0, 0).astype(jnp.float32), axis=0)


def vectors_of(blocks):
    return blocks.transpose(1, 0, 2).reshape(blocks.shape[1], -1)


def body(x_cols, diag_rows, theta, tiles, tile_rows, tile_cols, counts):
    core = lax.axis_index("c")
    slots, width = tiles.shape[2], tiles.shape[3]
    rows = jnp.pad(tile_rows[0, 0], (0, 32))
    cols = jnp.pad(tile_cols[0, 0], (0, 32))
    slot = jnp.arange(slots + 32, dtype=jnp.int32)
    used = slot < counts[0, 0]
    table = jnp.where(used, ((place(rows >> 2, core) << 2) | (rows & 3)) << 8 | cols, 128 << 8 | 64)
    table = jnp.where(slot == AT_ROW, lax.axis_index(ROW), table)
    table = jnp.where(slot == AT_COL, lax.axis_index(COL), table)
    table = jnp.where(slot == AT_CORE, core, table).astype(jnp.int32)

    smem = pl.BlockSpec(memory_space=pltpu.SMEM)
    vmem = pl.BlockSpec(memory_space=pltpu.VMEM)
    params = pltpu.CompilerParams(vmem_limit_bytes=16 * 1024 * 1024)
    cost = pl.CostEstimate(flops=2 * slots * 8 * width * width, bytes_accessed=4 << 20, transcendentals=0)
    f32 = functools.partial(jax.ShapeDtypeStruct, dtype=jnp.float32)

    tiles_here = tiles.reshape(slots // 2, 2 * width, width)
    lines = pl.pallas_call(
        prepare,
        out_shape=f32((8, width)),
        in_specs=[smem],
        out_specs=vmem,
        compiler_params=params,
        cost_estimate=pl.CostEstimate(flops=1 << 31, bytes_accessed=8 << 20, transcendentals=0),
    )(theta)

    own = x_cols.reshape(8, 4, width).transpose(1, 0, 2)
    x_all = to_all(own, ROW).reshape(64, 8, width)
    partial = pl.pallas_call(
        forward,
        out_shape=f32((128, 8, width)),
        in_specs=[smem, vmem, vmem, vmem],
        out_specs=vmem,
        scratch_shapes=[pltpu.VMEM((136, 8, width), jnp.float32)],
        compiler_params=params,
        cost_estimate=cost,
    )(table, tiles_here, lines, x_all)

    halves = lax.all_gather(partial[64:], "c")
    partial = partial[:64] + lax.dynamic_index_in_dim(halves, 1 - core, 0, keepdims=False)
    partial = sum_shares(partial, "y")
    diag_block = jnp.pad(diag_rows.reshape(1, 4, width), ((0, 0), (0, 4), (0, 0)))
    got = lax.all_gather(jnp.concatenate([partial, diag_block], axis=0), "zh")
    resid = jnp.sum(got[:, :16], axis=0)
    diag = got[:, 16, :4].reshape(16, 1, width)
    scaled = to_all((resid / diag).astype(jnp.bfloat16), "y").reshape(64, 8, width)
    scaled = lax.all_gather(scaled, "c", tiled=True)

    back = pl.pallas_call(
        backward,
        out_shape=f32((64, 8, width)),
        in_specs=[smem, vmem, vmem],
        out_specs=vmem,
        scratch_shapes=[pltpu.VMEM((72, 8, width), jnp.float32)],
        compiler_params=params,
        cost_estimate=cost,
    )(table, tiles_here, scaled)
    image = sum_shares(back, ROW)
    resid = lax.dynamic_slice_in_dim(resid, lax.axis_index("zh") * 4, 4, 0)
    return vectors_of(resid), vectors_of(image)


def solution(mesh):
    fine = Mesh(mesh.devices.reshape(4, 4, 4, 4, 2), ROW + COL)
    return jax.shard_map(
        body,
        mesh=fine,
        in_specs=(
            P(None, COL + ROW),
            P(ROW + COL),
            P(),
            P(ROW, COL, None, None, None),
            P(ROW, COL, None),
            P(ROW, COL, None),
            P(ROW, COL),
        ),
        out_specs=(P(None, ROW + COL), P(None, COL + ROW)),
        check_vma=False,
    )
```

```python
import functools

import jax
import jax.numpy as jnp
from jax import lax
from jax.experimental import pallas as pl
from jax.experimental.pallas import tpu as pltpu
from jax.sharding import Mesh, PartitionSpec as P

ROW = ("zl", "x")
COL = ("y", "zh", "c")
AT_ROW, AT_COL, AT_CORE = 96, 97, 98


def place(share, core):
    y, zh, c = share >> 3, (share >> 1) & 3, share & 1
    return ((c ^ core) << 4) | (y << 2) | zh


def prepare(theta_ref, diag_ref, lines_ref, block_ref):
    line = lax.broadcasted_iota(jnp.int32, lines_ref.shape, 0)
    lines = jnp.zeros(lines_ref.shape, jnp.float32)
    for n in range(8):
        lines = jnp.where(line == n, theta_ref[n], lines)
    lines_ref[...] = lines
    block_ref[:4] = diag_ref[...]
    block_ref[4:] = jnp.zeros((4, 128), jnp.float32)


def forward(table_ref, tiles_ref, lines_ref, x_ref, out_ref, total):
    total[...] = jnp.zeros_like(total)
    row, col = table_ref[AT_ROW], table_ref[AT_COL]

    @pl.when(row == col >> 1)
    def _():
        first = (col & 1) * 16

        def shift(s, carry):
            p = place(first + s, table_ref[AT_CORE]) * 4
            for j in range(4):
                total[p + j] = -lines_ref[...] * x_ref[s * 4 + j].astype(jnp.float32)
            return carry

        lax.fori_loop(0, 16, shift, 0)

    for i in range(48):
        v, w = table_ref[2 * i], table_ref[2 * i + 1]
        both = jnp.concatenate([x_ref[v & 63], x_ref[w & 63]], axis=0)
        part = lax.dot_general(
            both, tiles_ref[i], (((1,), (1,)), ((), ())), preferred_element_type=jnp.float32
        )
        total[v >> 8] = total[v >> 8] + part[:8, :128]
        total[w >> 8] = total[w >> 8] + part[8:, 128:]
    out_ref[...] = total[:128]


def backward(table_ref, tiles_ref, scaled_ref, out_ref, total):
    total[...] = jnp.zeros_like(total)
    half = table_ref[AT_CORE] << 6
    for i in range(48):
        v, w = table_ref[2 * i], table_ref[2 * i + 1]
        a, b = scaled_ref[((v >> 8) & 127) ^ half], scaled_ref[((w >> 8) & 127) ^ half]
        none = jnp.zeros_like(a)
        both = jnp.concatenate(
            [jnp.concatenate([a, none], axis=0), jnp.concatenate([none, b], axis=0)], axis=1
        )
        part = jnp.dot(both, tiles_ref[i], preferred_element_type=jnp.float32)
        total[v & 255] = total[v & 255] + part[:8]
        total[w & 255] = total[w & 255] + part[8:]
    out_ref[...] = total[:64].astype(out_ref.dtype)


def to_all(own, axes):
    copies = jnp.broadcast_to(own[None], (lax.axis_size(axes), *own.shape))
    return lax.all_to_all(copies, axes, 0, 0)


def sum_shares(parts, axes):
    n = lax.axis_size(axes)
    parts = parts.reshape(n, parts.shape[0] // n, *parts.shape[1:])
    return jnp.sum(lax.all_to_all(parts, axes, 0, 0).astype(jnp.float32), axis=0)


def gather_pairs(partial, diag, pairs):
    block = jnp.concatenate([partial, diag[None]], axis=0)
    return lax.all_gather(block, "zh", axis_index_groups=pairs)


def vectors_of(blocks):
    return blocks.transpose(1, 0, 2).reshape(blocks.shape[1], -1)


def body(x_cols, diag_rows, theta, tiles, tile_rows, tile_cols, counts):
    core = lax.axis_index("c")
    slots, width = tiles.shape[2], tiles.shape[3]
    rows = jnp.pad(tile_rows[0, 0], (0, 32))
    cols = jnp.pad(tile_cols[0, 0], (0, 32))
    slot = jnp.arange(slots + 32, dtype=jnp.int32)
    used = slot < counts[0, 0]
    table = jnp.where(used, ((place(rows >> 2, core) << 2) | (rows & 3)) << 8 | cols, 128 << 8 | 64)
    table = jnp.where(slot == AT_ROW, lax.axis_index(ROW), table)
    table = jnp.where(slot == AT_COL, lax.axis_index(COL), table)
    table = jnp.where(slot == AT_CORE, core, table).astype(jnp.int32)

    smem = pl.BlockSpec(memory_space=pltpu.SMEM)
    vmem = pl.BlockSpec(memory_space=pltpu.VMEM)
    params = pltpu.CompilerParams(vmem_limit_bytes=16 * 1024 * 1024)
    cost = pl.CostEstimate(flops=2 * slots * 8 * width * width, bytes_accessed=4 << 20, transcendentals=0)
    f32 = functools.partial(jax.ShapeDtypeStruct, dtype=jnp.float32)

    tiles_here = tiles.reshape(slots // 2, 2 * width, width)
    lines, diag = pl.pallas_call(
        prepare,
        out_shape=(f32((8, width)), f32((8, width))),
        in_specs=[smem, vmem],
        out_specs=(vmem, vmem),
        compiler_params=params,
        cost_estimate=pl.CostEstimate(flops=1 << 31, bytes_accessed=8 << 20, transcendentals=0),
    )(theta, diag_rows.reshape(4, width))

    own = x_cols.reshape(8, 4, width).transpose(1, 0, 2)
    x_all = to_all(own, ROW).reshape(64, 8, width)
    partial = pl.pallas_call(
        forward,
        out_shape=f32((128, 8, width)),
        in_specs=[smem, vmem, vmem, vmem],
        out_specs=vmem,
        scratch_shapes=[pltpu.VMEM((136, 8, width), jnp.float32)],
        compiler_params=params,
        cost_estimate=cost,
    )(table, tiles_here, lines, x_all)

    halves = lax.all_gather(partial[64:], "c")
    partial = partial[:64] + lax.dynamic_index_in_dim(halves, 1 - core, 0, keepdims=False)
    partial = sum_shares(partial, "y")
    got = gather_pairs(partial, diag, [[0, 1], [2, 3]])
    diag = got[:, 16, :4].reshape(8, width)
    got = gather_pairs(got[0, :16] + got[1, :16], diag, [[0, 3], [1, 2]])
    resid = got[0, :16] + got[1, :16]
    diag = got[:, 16].reshape(16, 1, width)
    scaled = to_all((resid / diag).astype(jnp.bfloat16), "y").reshape(64, 8, width)
    scaled = lax.all_gather(scaled, "c", tiled=True)

    back = pl.pallas_call(
        backward,
        out_shape=f32((64, 8, width)),
        in_specs=[smem, vmem, vmem],
        out_specs=vmem,
        scratch_shapes=[pltpu.VMEM((72, 8, width), jnp.float32)],
        compiler_params=params,
        cost_estimate=cost,
    )(table, tiles_here, scaled)
    image = sum_shares(back, ROW)
    resid = lax.dynamic_slice_in_dim(resid, lax.axis_index("zh") * 4, 4, 0)
    return vectors_of(resid), vectors_of(image)


def solution(mesh):
    fine = Mesh(mesh.devices.reshape(4, 4, 4, 4, 2), ROW + COL)
    return jax.shard_map(
        body,
        mesh=fine,
        in_specs=(
            P(None, COL + ROW),
            P(ROW + COL),
            P(),
            P(ROW, COL, None, None, None),
            P(ROW, COL, None),
            P(ROW, COL, None),
            P(ROW, COL),
        ),
        out_specs=(P(None, ROW + COL), P(None, COL + ROW)),
        check_vma=False,
    )
```

```python
import functools

import jax
import jax.numpy as jnp
from jax import lax
from jax.experimental import pallas as pl
from jax.experimental.pallas import tpu as pltpu
from jax.sharding import Mesh, PartitionSpec as P

ROW = ("zl", "x")
COL = ("y", "zh", "c")
BACK = jnp.bfloat16
AT_ROW, AT_COL, AT_CORE, AT_ZH, AT_THETA = 96, 97, 98, 99, 104


def place(share, core):
    y, zh, c = share >> 3, (share >> 1) & 3, share & 1
    return ((c ^ core) << 4) | (y << 2) | zh


def settle(table_ref, out_ref):
    out_ref[...] = table_ref[...]


def number(table_ref, at):
    return table_ref[at].astype(jnp.int32)


def forward(table_ref, tiles_ref, x_ref, out_ref, total):
    total[...] = jnp.zeros_like(total)
    row, col = number(table_ref, AT_ROW), number(table_ref, AT_COL)

    @pl.when(row == col >> 1)
    def _():
        first = (col & 1) * 16
        line = lax.broadcasted_iota(jnp.int32, (8, 128), 0)
        theta = jnp.zeros((8, 128), jnp.float32)
        for n in range(8):
            theta = jnp.where(line == n, table_ref[AT_THETA + n], theta)

        def shift(s, carry):
            p = place(first + s, col & 1) * 4
            for j in range(4):
                total[p + j] = -theta * x_ref[s * 4 + j].astype(jnp.float32)
            return carry

        lax.fori_loop(0, 16, shift, 0)

    for i in range(48):
        v, w = number(table_ref, 2 * i), number(table_ref, 2 * i + 1)
        both = jnp.concatenate([x_ref[v & 63], x_ref[w & 63]], axis=0)
        part = lax.dot_general(
            both, tiles_ref[i], (((1,), (1,)), ((), ())), preferred_element_type=jnp.float32
        )
        total[v >> 8] = total[v >> 8] + part[:8, :128]
        total[w >> 8] = total[w >> 8] + part[8:, 128:]
    out_ref[...] = total[:128]


def backward(table_ref, tiles_ref, scaled_ref, resid_ref, out_ref, own_ref, total, sem):
    own = resid_ref.at[pl.ds(number(table_ref, AT_ZH) * 4, 4)]
    copy = pltpu.make_async_copy(own, own_ref, sem)
    copy.start()
    total[...] = jnp.zeros_like(total)
    half = number(table_ref, AT_CORE) << 6
    for i in range(48):
        v, w = number(table_ref, 2 * i), number(table_ref, 2 * i + 1)
        a, b = scaled_ref[((v >> 8) & 127) ^ half], scaled_ref[((w >> 8) & 127) ^ half]
        none = jnp.zeros_like(a)
        both = jnp.concatenate(
            [jnp.concatenate([a, none], axis=0), jnp.concatenate([none, b], axis=0)], axis=1
        )
        part = jnp.dot(both, tiles_ref[i], preferred_element_type=jnp.float32)
        total[v & 255] = total[v & 255] + part[:8]
        total[w & 255] = total[w & 255] + part[8:]
    out_ref[...] = total[:64].astype(out_ref.dtype)
    copy.wait()


def to_all(own, axes):
    copies = jnp.broadcast_to(own[None], (lax.axis_size(axes), *own.shape))
    return lax.all_to_all(copies, axes, 0, 0)


def sum_shares(parts, axes):
    n = lax.axis_size(axes)
    parts = parts.reshape(n, parts.shape[0] // n, *parts.shape[1:])
    return jnp.sum(lax.all_to_all(parts, axes, 0, 0).astype(jnp.float32), axis=0)


def gather_pairs(partial, diag, pairs):
    diag = jnp.pad(diag, ((0, 0), (0, 8 - diag.shape[1]), (0, 0)))
    return lax.all_gather(jnp.concatenate([partial, diag], axis=0), "zh", axis_index_groups=pairs)


def vectors_of(blocks):
    return blocks.transpose(1, 0, 2).reshape(blocks.shape[1], -1)


def body(x_cols, diag_rows, theta, tiles, tile_rows, tile_cols, counts):
    core = lax.axis_index("c")
    slots, width = tiles.shape[2], tiles.shape[3]
    rows = jnp.pad(tile_rows[0, 0], (0, 32))
    cols = jnp.pad(tile_cols[0, 0], (0, 32))
    slot = jnp.arange(slots + 32, dtype=jnp.int32)
    used = slot < counts[0, 0]
    table = jnp.where(used, ((place(rows >> 2, core) << 2) | (rows & 3)) << 8 | cols, 128 << 8 | 64)
    table = jnp.where(slot == AT_ROW, lax.axis_index(ROW), table)
    table = jnp.where(slot == AT_COL, lax.axis_index(COL), table)
    table = jnp.where(slot == AT_CORE, core, table)
    table = jnp.where(slot == AT_ZH, lax.axis_index("zh"), table).astype(jnp.float32)
    table = jnp.where(slot < AT_THETA, table, jnp.pad(theta, (AT_THETA, 16)))

    smem = pl.BlockSpec(memory_space=pltpu.SMEM)
    vmem = pl.BlockSpec(memory_space=pltpu.VMEM)
    params = pltpu.CompilerParams(vmem_limit_bytes=16 * 1024 * 1024)
    cost = pl.CostEstimate(flops=2 * slots * 8 * width * width, bytes_accessed=4 << 20, transcendentals=0)
    f32 = functools.partial(jax.ShapeDtypeStruct, dtype=jnp.float32)

    tiles_here = tiles.reshape(slots // 2, 2 * width, width)
    table = pl.pallas_call(
        settle,
        out_shape=f32(table.shape),
        in_specs=[vmem],
        out_specs=vmem,
        compiler_params=params,
        cost_estimate=pl.CostEstimate(flops=1 << 31, bytes_accessed=8 << 20, transcendentals=0),
    )(table)

    own = x_cols.reshape(8, 4, width).transpose(1, 0, 2)
    x_all = to_all(own, ROW).reshape(64, 8, width)
    partial = pl.pallas_call(
        forward,
        out_shape=f32((128, 8, width)),
        in_specs=[smem, vmem, vmem],
        out_specs=vmem,
        scratch_shapes=[pltpu.VMEM((136, 8, width), jnp.float32)],
        compiler_params=params,
        cost_estimate=cost,
    )(table, tiles_here, x_all)

    halves = lax.all_gather(partial[64:], "c")
    partial = partial[:64] + lax.dynamic_index_in_dim(halves, 1 - core, 0, keepdims=False)
    partial = sum_shares(partial, "y")
    got = gather_pairs(partial, diag_rows.reshape(1, 4, width), [[0, 1], [2, 3]])
    diag = got[:, 16, :4].reshape(1, 8, width)
    got = gather_pairs(got[0, :16] + got[1, :16], diag, [[0, 3], [1, 2]])
    resid = got[0, :16] + got[1, :16]
    diag = got[:, 16].reshape(16, 1, width)
    scaled = to_all((resid / diag).astype(jnp.bfloat16), "y").reshape(64, 8, width)
    scaled = lax.all_gather(scaled, "c", tiled=True)

    back, resid = pl.pallas_call(
        backward,
        out_shape=(jax.ShapeDtypeStruct((64, 8, width), BACK), f32((4, 8, width))),
        in_specs=[smem, vmem, vmem, vmem],
        out_specs=(vmem, pl.BlockSpec(memory_space=pl.ANY)),
        scratch_shapes=[pltpu.VMEM((72, 8, width), jnp.float32), pltpu.SemaphoreType.DMA],
        compiler_params=params,
        cost_estimate=cost,
    )(table, tiles_here, scaled, resid)
    return vectors_of(resid), vectors_of(sum_shares(back, ROW))


def solution(mesh):
    fine = Mesh(mesh.devices.reshape(4, 4, 4, 4, 2), ROW + COL)
    return jax.shard_map(
        body,
        mesh=fine,
        in_specs=(
            P(None, COL + ROW),
            P(ROW + COL),
            P(),
            P(ROW, COL, None, None, None),
            P(ROW, COL, None),
            P(ROW, COL, None),
            P(ROW, COL),
        ),
        out_specs=(P(None, ROW + COL), P(None, COL + ROW)),
        check_vma=False,
    )
```

```python
import functools

import jax
import jax.numpy as jnp
from jax import lax
from jax.experimental import pallas as pl
from jax.experimental.pallas import tpu as pltpu
from jax.sharding import Mesh, PartitionSpec as P

ROW = ("zl", "x")
COL = ("y", "zh", "c")
BACK = jnp.bfloat16
AT_ROW, AT_COL, AT_CORE, AT_ZH, AT_THETA = 96, 97, 98, 99, 104


def place(share, core):
    y, zh, c = share >> 3, (share >> 1) & 3, share & 1
    return (y << 3) | ((c ^ core) << 2) | zh


def settle(table_ref, out_ref):
    out_ref[...] = table_ref[...]


def number(table_ref, at):
    return table_ref[at].astype(jnp.int32)


def forward(table_ref, tiles_ref, x_ref, out_ref, total):
    total[...] = jnp.zeros_like(total)
    row, col = number(table_ref, AT_ROW), number(table_ref, AT_COL)

    @pl.when(row == col >> 1)
    def _():
        first = (col & 1) * 16
        line = lax.broadcasted_iota(jnp.int32, (8, 128), 0)
        theta = jnp.zeros((8, 128), jnp.float32)
        for n in range(8):
            theta = jnp.where(line == n, table_ref[AT_THETA + n], theta)

        def shift(s, carry):
            p = place(first + s, col & 1) * 4
            for j in range(4):
                total[p + j] = -theta * x_ref[s * 4 + j].astype(jnp.float32)
            return carry

        lax.fori_loop(0, 16, shift, 0)

    for i in range(48):
        v, w = number(table_ref, 2 * i), number(table_ref, 2 * i + 1)
        both = jnp.concatenate([x_ref[v & 63], x_ref[w & 63]], axis=0)
        part = lax.dot_general(
            both, tiles_ref[i], (((1,), (1,)), ((), ())), preferred_element_type=jnp.float32
        )
        total[v >> 8] = total[v >> 8] + part[:8, :128]
        total[w >> 8] = total[w >> 8] + part[8:, 128:]
    out_ref[...] = total[:128]


def backward(table_ref, tiles_ref, scaled_ref, resid_ref, out_ref, own_ref, total, sem):
    own = resid_ref.at[pl.ds(number(table_ref, AT_ZH) * 4, 4)]
    copy = pltpu.make_async_copy(own, own_ref, sem)
    copy.start()
    total[...] = jnp.zeros_like(total)
    half = number(table_ref, AT_CORE) << 4
    for i in range(48):
        v, w = number(table_ref, 2 * i), number(table_ref, 2 * i + 1)
        a, b = scaled_ref[((v >> 8) & 127) ^ half], scaled_ref[((w >> 8) & 127) ^ half]
        none = jnp.zeros_like(a)
        both = jnp.concatenate(
            [jnp.concatenate([a, none], axis=0), jnp.concatenate([none, b], axis=0)], axis=1
        )
        part = jnp.dot(both, tiles_ref[i], preferred_element_type=jnp.float32)
        total[v & 255] = total[v & 255] + part[:8]
        total[w & 255] = total[w & 255] + part[8:]
    out_ref[...] = total[:64].astype(out_ref.dtype)
    copy.wait()


def to_all(own, axes):
    copies = jnp.broadcast_to(own[None], (lax.axis_size(axes), *own.shape))
    return lax.all_to_all(copies, axes, 0, 0)


def sum_shares(parts, axes):
    n = lax.axis_size(axes)
    parts = parts.reshape(n, parts.shape[0] // n, *parts.shape[1:])
    return jnp.sum(lax.all_to_all(parts, axes, 0, 0).astype(jnp.float32), axis=0)


def gather_pairs(partial, diag, pairs):
    diag = jnp.pad(diag, ((0, 0), (0, 8 - diag.shape[1]), (0, 0)))
    return lax.all_gather(jnp.concatenate([partial, diag], axis=0), "zh", axis_index_groups=pairs)


def vectors_of(blocks):
    return blocks.transpose(1, 0, 2).reshape(blocks.shape[1], -1)


def body(x_cols, diag_rows, theta, tiles, tile_rows, tile_cols, counts):
    core = lax.axis_index("c")
    slots, width = tiles.shape[2], tiles.shape[3]
    rows = jnp.pad(tile_rows[0, 0], (0, 32))
    cols = jnp.pad(tile_cols[0, 0], (0, 32))
    slot = jnp.arange(slots + 32, dtype=jnp.int32)
    used = slot < counts[0, 0]
    table = jnp.where(used, ((place(rows >> 2, core) << 2) | (rows & 3)) << 8 | cols, 128 << 8 | 64)
    table = jnp.where(slot == AT_ROW, lax.axis_index(ROW), table)
    table = jnp.where(slot == AT_COL, lax.axis_index(COL), table)
    table = jnp.where(slot == AT_CORE, core, table)
    table = jnp.where(slot == AT_ZH, lax.axis_index("zh"), table).astype(jnp.float32)
    table = jnp.where(slot < AT_THETA, table, jnp.pad(theta, (AT_THETA, 16)))

    smem = pl.BlockSpec(memory_space=pltpu.SMEM)
    vmem = pl.BlockSpec(memory_space=pltpu.VMEM)
    params = pltpu.CompilerParams(vmem_limit_bytes=16 * 1024 * 1024)
    cost = pl.CostEstimate(flops=2 * slots * 8 * width * width, bytes_accessed=4 << 20, transcendentals=0)
    f32 = functools.partial(jax.ShapeDtypeStruct, dtype=jnp.float32)

    tiles_here = tiles.reshape(slots // 2, 2 * width, width)
    table = pl.pallas_call(
        settle,
        out_shape=f32(table.shape),
        in_specs=[vmem],
        out_specs=vmem,
        compiler_params=params,
        cost_estimate=pl.CostEstimate(flops=1 << 31, bytes_accessed=8 << 20, transcendentals=0),
    )(table)

    own = x_cols.reshape(8, 4, width).transpose(1, 0, 2)
    x_all = to_all(own, ROW).reshape(64, 8, width)
    partial = pl.pallas_call(
        forward,
        out_shape=f32((128, 8, width)),
        in_specs=[smem, vmem, vmem],
        out_specs=vmem,
        scratch_shapes=[pltpu.VMEM((136, 8, width), jnp.float32)],
        compiler_params=params,
        cost_estimate=cost,
    )(table, tiles_here, x_all)

    partial = partial.reshape(4, 2, 16, 8, width)
    halves = lax.all_gather(partial[:, 1], "c")
    partial = partial[:, 0] + lax.dynamic_index_in_dim(halves, 1 - core, 0, keepdims=False)
    partial = jnp.sum(lax.all_to_all(partial, "y", 0, 0), axis=0)
    got = gather_pairs(partial, diag_rows.reshape(1, 4, width), [[0, 3], [1, 2]])
    diag = got[:, 16, :4].reshape(1, 8, width)
    got = gather_pairs(got[0, :16] + got[1, :16], diag, [[0, 1], [3, 2]])
    resid = got[0, :16] + got[1, :16]
    diag = got[:, 16]
    diag = jnp.concatenate([diag[0, :4], diag[1], diag[0, 4:]], axis=0).reshape(16, 1, width)
    scaled = to_all((resid / diag).astype(jnp.bfloat16), ("y", "c")).reshape(128, 8, width)

    back, resid = pl.pallas_call(
        backward,
        out_shape=(jax.ShapeDtypeStruct((64, 8, width), BACK), f32((4, 8, width))),
        in_specs=[smem, vmem, vmem, vmem],
        out_specs=(vmem, pl.BlockSpec(memory_space=pl.ANY)),
        scratch_shapes=[pltpu.VMEM((72, 8, width), jnp.float32), pltpu.SemaphoreType.DMA],
        compiler_params=params,
        cost_estimate=cost,
    )(table, tiles_here, scaled, resid)
    return vectors_of(resid), vectors_of(sum_shares(back, ROW))


def solution(mesh):
    fine = Mesh(mesh.devices.reshape(4, 4, 4, 4, 2), ROW + COL)
    return jax.shard_map(
        body,
        mesh=fine,
        in_specs=(
            P(None, COL + ROW),
            P(ROW + COL),
            P(),
            P(ROW, COL, None, None, None),
            P(ROW, COL, None),
            P(ROW, COL, None),
            P(ROW, COL),
        ),
        out_specs=(P(None, ROW + COL), P(None, COL + ROW)),
        check_vma=False,
    )
```

```python
import functools

import jax
import jax.numpy as jnp
from jax import lax
from jax.experimental import pallas as pl
from jax.experimental.pallas import tpu as pltpu
from jax.sharding import Mesh, PartitionSpec as P

ROW = ("zl", "x")
COL = ("y", "zh", "c")
BACK = jnp.bfloat16
AT_ROW, AT_COL, AT_CORE, AT_ZH, AT_THETA = 96, 97, 98, 99, 104


def place(share, core):
    y, zh, c = share >> 3, (share >> 1) & 3, share & 1
    return (y << 3) | ((c ^ core) << 2) | zh


def settle(table_ref, out_ref):
    out_ref[...] = table_ref[...]


def number(table_ref, at):
    return table_ref[at].astype(jnp.int32)


def forward(table_ref, tiles_ref, x_ref, out_ref, total):
    total[...] = jnp.zeros_like(total)
    row, col = number(table_ref, AT_ROW), number(table_ref, AT_COL)

    @pl.when(row == col >> 1)
    def _():
        first = (col & 1) * 16
        line = lax.broadcasted_iota(jnp.int32, (8, 128), 0)
        theta = jnp.zeros((8, 128), jnp.float32)
        for n in range(8):
            theta = jnp.where(line == n, table_ref[AT_THETA + n], theta)

        def shift(s, carry):
            p = place(first + s, col & 1) * 4
            for j in range(4):
                total[p + j] = -theta * x_ref[s * 4 + j].astype(jnp.float32)
            return carry

        lax.fori_loop(0, 16, shift, 0)

    for i in range(48):
        v, w = number(table_ref, 2 * i), number(table_ref, 2 * i + 1)
        both = jnp.concatenate([x_ref[v & 63], x_ref[w & 63]], axis=0)
        part = lax.dot_general(
            both, tiles_ref[i], (((1,), (1,)), ((), ())), preferred_element_type=jnp.float32
        )
        total[v >> 8] = total[v >> 8] + part[:8, :128]
        total[w >> 8] = total[w >> 8] + part[8:, 128:]
    out_ref[...] = total[:128]


def backward(table_ref, tiles_ref, scaled_ref, resid_ref, out_ref, own_ref, total):
    own_ref[...] = resid_ref[pl.ds(number(table_ref, AT_ZH) * 4, 4)]
    total[...] = jnp.zeros_like(total)
    half = number(table_ref, AT_CORE) << 4
    for i in range(48):
        v, w = number(table_ref, 2 * i), number(table_ref, 2 * i + 1)
        a, b = scaled_ref[((v >> 8) & 127) ^ half], scaled_ref[((w >> 8) & 127) ^ half]
        none = jnp.zeros_like(a)
        both = jnp.concatenate(
            [jnp.concatenate([a, none], axis=0), jnp.concatenate([none, b], axis=0)], axis=1
        )
        part = jnp.dot(both, tiles_ref[i], preferred_element_type=jnp.float32)
        total[v & 255] = total[v & 255] + part[:8]
        total[w & 255] = total[w & 255] + part[8:]
    out_ref[...] = total[:64].astype(out_ref.dtype)


def finish(parts_ref, own_ref, image_ref, resid_ref):
    resid_ref[...] = own_ref[...]
    image_ref[...] = jnp.sum(parts_ref[...].astype(jnp.float32), axis=0)


def to_all(own, axes):
    copies = jnp.broadcast_to(own[None], (lax.axis_size(axes), *own.shape))
    return lax.all_to_all(copies, axes, 0, 0)


def gather_pairs(partial, diag, pairs):
    diag = jnp.pad(diag, ((0, 0), (0, 8 - diag.shape[1]), (0, 0)))
    return lax.all_gather(jnp.concatenate([partial, diag], axis=0), "zh", axis_index_groups=pairs)


def vectors_of(blocks):
    return blocks.transpose(1, 0, 2).reshape(blocks.shape[1], -1)


def body(x_cols, diag_rows, theta, tiles, tile_rows, tile_cols, counts):
    core = lax.axis_index("c")
    slots, width = tiles.shape[2], tiles.shape[3]
    rows = jnp.pad(tile_rows[0, 0], (0, 32))
    cols = jnp.pad(tile_cols[0, 0], (0, 32))
    slot = jnp.arange(slots + 32, dtype=jnp.int32)
    used = slot < counts[0, 0]
    table = jnp.where(used, ((place(rows >> 2, core) << 2) | (rows & 3)) << 8 | cols, 128 << 8 | 64)
    table = jnp.where(slot == AT_ROW, lax.axis_index(ROW), table)
    table = jnp.where(slot == AT_COL, lax.axis_index(COL), table)
    table = jnp.where(slot == AT_CORE, core, table)
    table = jnp.where(slot == AT_ZH, lax.axis_index("zh"), table).astype(jnp.float32)
    table = jnp.where(slot < AT_THETA, table, jnp.pad(theta, (AT_THETA, 16)))

    smem = pl.BlockSpec(memory_space=pltpu.SMEM)
    vmem = pl.BlockSpec(memory_space=pltpu.VMEM)
    params = pltpu.CompilerParams(vmem_limit_bytes=16 * 1024 * 1024)
    cost = pl.CostEstimate(flops=2 * slots * 8 * width * width, bytes_accessed=4 << 20, transcendentals=0)
    f32 = functools.partial(jax.ShapeDtypeStruct, dtype=jnp.float32)

    tiles_here = tiles.reshape(slots // 2, 2 * width, width)
    table = pl.pallas_call(
        settle,
        out_shape=f32(table.shape),
        in_specs=[vmem],
        out_specs=vmem,
        compiler_params=params,
        cost_estimate=pl.CostEstimate(flops=1 << 31, bytes_accessed=8 << 20, transcendentals=0),
    )(table)

    own = x_cols.reshape(8, 4, width).transpose(1, 0, 2)
    x_all = to_all(own, ROW).reshape(64, 8, width)
    partial = pl.pallas_call(
        forward,
        out_shape=f32((128, 8, width)),
        in_specs=[smem, vmem, vmem],
        out_specs=vmem,
        scratch_shapes=[pltpu.VMEM((136, 8, width), jnp.float32)],
        compiler_params=params,
        cost_estimate=cost,
    )(table, tiles_here, x_all)

    partial = partial.reshape(4, 2, 16, 8, width)
    halves = lax.all_gather(partial[:, 1], "c")
    partial = partial[:, 0] + lax.dynamic_index_in_dim(halves, 1 - core, 0, keepdims=False)
    partial = jnp.sum(lax.all_to_all(partial, "y", 0, 0), axis=0)
    got = gather_pairs(partial, diag_rows.reshape(1, 4, width), [[0, 3], [1, 2]])
    diag = got[:, 16, :4].reshape(1, 8, width)
    got = gather_pairs(got[0, :16] + got[1, :16], diag, [[0, 1], [3, 2]])
    resid = got[0, :16] + got[1, :16]
    diag = got[:, 16]
    diag = jnp.concatenate([diag[0, :4], diag[1], diag[0, 4:]], axis=0).reshape(16, 1, width)
    scaled = to_all((resid / diag).astype(jnp.bfloat16), ("y", "c")).reshape(128, 8, width)

    back, resid = pl.pallas_call(
        backward,
        out_shape=(jax.ShapeDtypeStruct((64, 8, width), BACK), pltpu.VMEM((4, 8, width), jnp.float32)),
        in_specs=[smem, vmem, vmem, vmem],
        out_specs=(vmem, vmem),
        scratch_shapes=[pltpu.VMEM((72, 8, width), jnp.float32)],
        compiler_params=params,
        cost_estimate=cost,
    )(table, tiles_here, scaled, resid)
    image, resid = pl.pallas_call(
        finish,
        out_shape=(f32((4, 8, width)), f32((4, 8, width))),
        in_specs=[vmem, vmem],
        out_specs=(vmem, vmem),
        compiler_params=params,
    )(lax.all_to_all(back.reshape(16, 4, 8, width), ROW, 0, 0), resid)
    return vectors_of(resid), vectors_of(image)


def solution(mesh):
    fine = Mesh(mesh.devices.reshape(4, 4, 4, 4, 2), ROW + COL)
    return jax.shard_map(
        body,
        mesh=fine,
        in_specs=(
            P(None, COL + ROW),
            P(ROW + COL),
            P(),
            P(ROW, COL, None, None, None),
            P(ROW, COL, None),
            P(ROW, COL, None),
            P(ROW, COL),
        ),
        out_specs=(P(None, ROW + COL), P(None, COL + ROW)),
        check_vma=False,
    )
```

```python
import functools

import jax
import jax.numpy as jnp
from jax import lax
from jax.experimental import pallas as pl
from jax.experimental.pallas import tpu as pltpu
from jax.sharding import Mesh, PartitionSpec as P

ROW = ("zl", "x")
COL = ("y", "zh", "c")
BACK = jnp.bfloat16
AT_ROW, AT_COL, AT_CORE, AT_ZH, AT_THETA = 96, 97, 98, 99, 104


def place(share, core):
    y, zh, c = share >> 3, (share >> 1) & 3, share & 1
    return (y << 3) | ((c ^ core) << 2) | zh


def settle(table_ref, out_ref):
    out_ref[...] = table_ref[...]


def number(table_ref, at):
    return table_ref[at].astype(jnp.int32)


def forward(table_ref, tiles_ref, x_ref, own_ref, other_ref, total):
    total[...] = jnp.zeros_like(total)
    row, col = number(table_ref, AT_ROW), number(table_ref, AT_COL)

    @pl.when(row == col >> 1)
    def _():
        first = (col & 1) * 16
        line = lax.broadcasted_iota(jnp.int32, (8, 128), 0)
        theta = jnp.zeros((8, 128), jnp.float32)
        for n in range(8):
            theta = jnp.where(line == n, table_ref[AT_THETA + n], theta)

        for s in range(16):
            p = place(first + s, col & 1) * 4
            for j in range(4):
                total[p + j] = -theta * x_ref[s * 4 + j].astype(jnp.float32)

    parts = []
    for i in range(48):
        v, w = number(table_ref, 2 * i), number(table_ref, 2 * i + 1)
        both = jnp.concatenate([x_ref[v & 63], x_ref[w & 63]], axis=0)
        part = lax.dot_general(
            both, tiles_ref[i], (((1,), (1,)), ((), ())), preferred_element_type=jnp.float32
        )
        parts += [(v >> 8, part[:8, :128]), (w >> 8, part[8:, 128:])]
        if len(parts) == 16:
            for p, part in parts:
                total[p] = total[p] + part
            parts = []
    for y in range(4):
        own_ref[y] = total[y * 32 : y * 32 + 16]
        other_ref[y] = total[y * 32 + 16 : y * 32 + 32]


def backward(table_ref, tiles_ref, scaled_ref, resid_ref, out_ref, own_ref, total):
    own_ref[...] = resid_ref[pl.ds(number(table_ref, AT_ZH) * 4, 4)]
    total[...] = jnp.zeros_like(total)
    half = number(table_ref, AT_CORE) << 4
    for i in range(48):
        v, w = number(table_ref, 2 * i), number(table_ref, 2 * i + 1)
        a, b = scaled_ref[((v >> 8) & 127) ^ half], scaled_ref[((w >> 8) & 127) ^ half]
        none = jnp.zeros_like(a)
        both = jnp.concatenate(
            [jnp.concatenate([a, none], axis=0), jnp.concatenate([none, b], axis=0)], axis=1
        )
        part = jnp.dot(both, tiles_ref[i], preferred_element_type=jnp.float32)
        total[v & 255] = total[v & 255] + part[:8]
        total[w & 255] = total[w & 255] + part[8:]
    out_ref[...] = total[:64].astype(out_ref.dtype)


def finish(parts_ref, own_ref, image_ref, resid_ref):
    resid_ref[...] = own_ref[...]
    image_ref[...] = jnp.sum(parts_ref[...].astype(jnp.float32), axis=0)


def to_all(own, axes):
    copies = jnp.broadcast_to(own[None], (lax.axis_size(axes), *own.shape))
    return lax.all_to_all(copies, axes, 0, 0)


def gather_pairs(partial, diag, pairs):
    diag = jnp.pad(diag, ((0, 0), (0, 8 - diag.shape[1]), (0, 0)))
    return lax.all_gather(jnp.concatenate([partial, diag], axis=0), "zh", axis_index_groups=pairs)


def vectors_of(blocks):
    return blocks.transpose(1, 0, 2).reshape(blocks.shape[1], -1)


def body(x_cols, diag_rows, theta, tiles, tile_rows, tile_cols, counts):
    core = lax.axis_index("c")
    slots, width = tiles.shape[2], tiles.shape[3]
    rows = jnp.pad(tile_rows[0, 0], (0, 32))
    cols = jnp.pad(tile_cols[0, 0], (0, 32))
    slot = jnp.arange(slots + 32, dtype=jnp.int32)
    used = slot < counts[0, 0]
    table = jnp.where(used, ((place(rows >> 2, core) << 2) | (rows & 3)) << 8 | cols, 128 << 8 | 64)
    table = jnp.where(slot == AT_ROW, lax.axis_index(ROW), table)
    table = jnp.where(slot == AT_COL, lax.axis_index(COL), table)
    table = jnp.where(slot == AT_CORE, core, table)
    table = jnp.where(slot == AT_ZH, lax.axis_index("zh"), table).astype(jnp.float32)
    table = jnp.where(slot < AT_THETA, table, jnp.pad(theta, (AT_THETA, 16)))

    smem = pl.BlockSpec(memory_space=pltpu.SMEM)
    vmem = pl.BlockSpec(memory_space=pltpu.VMEM)
    params = pltpu.CompilerParams(vmem_limit_bytes=16 * 1024 * 1024)
    cost = pl.CostEstimate(flops=2 * slots * 8 * width * width, bytes_accessed=4 << 20, transcendentals=0)
    f32 = functools.partial(jax.ShapeDtypeStruct, dtype=jnp.float32)

    tiles_here = tiles.reshape(slots // 2, 2 * width, width)
    table = pl.pallas_call(
        settle,
        out_shape=f32(table.shape),
        in_specs=[vmem],
        out_specs=vmem,
        compiler_params=params,
        cost_estimate=pl.CostEstimate(flops=1 << 31, bytes_accessed=8 << 20, transcendentals=0),
    )(table)

    own = x_cols.reshape(8, 4, width).transpose(1, 0, 2)
    x_all = to_all(own, ROW).reshape(64, 8, width)
    partial, other = pl.pallas_call(
        forward,
        out_shape=(f32((4, 16, 8, width)), f32((4, 16, 8, width))),
        in_specs=[smem, vmem, vmem],
        out_specs=(vmem, vmem),
        scratch_shapes=[pltpu.VMEM((136, 8, width), jnp.float32)],
        compiler_params=params,
        cost_estimate=cost,
    )(table, tiles_here, x_all)

    halves = lax.all_gather(other, "c")
    partial = partial + lax.dynamic_index_in_dim(halves, 1 - core, 0, keepdims=False)
    partial = jnp.sum(lax.all_to_all(partial, "y", 0, 0), axis=0)
    got = gather_pairs(partial, diag_rows.reshape(1, 4, width), [[0, 3], [1, 2]])
    diag = got[:, 16, :4].reshape(1, 8, width)
    got = gather_pairs(got[0, :16] + got[1, :16], diag, [[0, 1], [3, 2]])
    resid = got[0, :16] + got[1, :16]
    diag = got[:, 16]
    diag = jnp.concatenate([diag[0, :4], diag[1], diag[0, 4:]], axis=0).reshape(16, 1, width)
    scaled = to_all((resid / diag).astype(jnp.bfloat16), ("y", "c")).reshape(128, 8, width)

    back, resid = pl.pallas_call(
        backward,
        out_shape=(jax.ShapeDtypeStruct((64, 8, width), BACK), pltpu.VMEM((4, 8, width), jnp.float32)),
        in_specs=[smem, vmem, vmem, vmem],
        out_specs=(vmem, vmem),
        scratch_shapes=[pltpu.VMEM((72, 8, width), jnp.float32)],
        compiler_params=params,
        cost_estimate=cost,
    )(table, tiles_here, scaled, resid)
    image, resid = pl.pallas_call(
        finish,
        out_shape=(f32((4, 8, width)), f32((4, 8, width))),
        in_specs=[vmem, vmem],
        out_specs=(vmem, vmem),
        compiler_params=params,
    )(lax.all_to_all(back.reshape(16, 4, 8, width), ROW, 0, 0), resid)
    return vectors_of(resid), vectors_of(image)


def solution(mesh):
    fine = Mesh(mesh.devices.reshape(4, 4, 4, 4, 2), ROW + COL)
    return jax.shard_map(
        body,
        mesh=fine,
        in_specs=(
            P(None, COL + ROW),
            P(ROW + COL),
            P(),
            P(ROW, COL, None, None, None),
            P(ROW, COL, None),
            P(ROW, COL, None),
            P(ROW, COL),
        ),
        out_specs=(P(None, ROW + COL), P(None, COL + ROW)),
        check_vma=False,
    )
```

```python
import functools

import jax
import jax.numpy as jnp
from jax import lax
from jax.experimental import pallas as pl
from jax.experimental.pallas import tpu as pltpu
from jax.sharding import Mesh, PartitionSpec as P

ROW = ("zl", "x")
COL = ("y", "zh", "c")
BACK = jnp.bfloat16
AT_ROW, AT_COL, AT_CORE, AT_ZH, AT_THETA = 96, 97, 98, 99, 104


def place(share, core):
    y, zh, c = share >> 3, (share >> 1) & 3, share & 1
    return (y << 3) | ((c ^ core) << 2) | zh


def settle(table_ref, out_ref):
    out_ref[...] = table_ref[...]


def number(table_ref, at):
    return table_ref[at].astype(jnp.int32)


def forward(table_in, tiles_ref, x_ref, out_ref, total, table_ref, sem):
    copy = pltpu.make_async_copy(table_in, table_ref, sem)
    copy.start()
    total[...] = jnp.zeros_like(total)
    copy.wait()
    row, col = number(table_ref, AT_ROW), number(table_ref, AT_COL)

    @pl.when(row == col >> 1)
    def _():
        first = (col & 1) * 16
        line = lax.broadcasted_iota(jnp.int32, (8, 128), 0)
        theta = jnp.zeros((8, 128), jnp.float32)
        for n in range(8):
            theta = jnp.where(line == n, table_ref[AT_THETA + n], theta)

        def shift(s, carry):
            p = place(first + s, col & 1) * 4
            for j in range(4):
                total[p + j] = -theta * x_ref[s * 4 + j].astype(jnp.float32)
            return carry

        lax.fori_loop(0, 16, shift, 0)

    for i in range(48):
        v, w = number(table_ref, 2 * i), number(table_ref, 2 * i + 1)
        both = jnp.concatenate([x_ref[v & 63], x_ref[w & 63]], axis=0)
        part = lax.dot_general(
            both, tiles_ref[i], (((1,), (1,)), ((), ())), preferred_element_type=jnp.float32
        )
        total[v >> 8] = total[v >> 8] + part[:8, :128]
        total[w >> 8] = total[w >> 8] + part[8:, 128:]
    out_ref[...] = total[:128]


def backward(table_in, tiles_ref, scaled_ref, resid_ref, out_ref, own_ref, total, table_ref, sem):
    copy = pltpu.make_async_copy(table_in, table_ref, sem)
    copy.start()
    total[...] = jnp.zeros_like(total)
    copy.wait()
    own_ref[...] = resid_ref[pl.ds(number(table_ref, AT_ZH) * 4, 4)]
    half = number(table_ref, AT_CORE) << 4
    for i in range(48):
        v, w = number(table_ref, 2 * i), number(table_ref, 2 * i + 1)
        a, b = scaled_ref[((v >> 8) & 127) ^ half], scaled_ref[((w >> 8) & 127) ^ half]
        none = jnp.zeros_like(a)
        both = jnp.concatenate(
            [jnp.concatenate([a, none], axis=0), jnp.concatenate([none, b], axis=0)], axis=1
        )
        part = jnp.dot(both, tiles_ref[i], preferred_element_type=jnp.float32)
        total[v & 255] = total[v & 255] + part[:8]
        total[w & 255] = total[w & 255] + part[8:]
    out_ref[...] = total[:64].astype(out_ref.dtype)


def finish(parts_ref, own_ref, image_ref, resid_ref):
    resid_ref[...] = own_ref[...]
    image_ref[...] = jnp.sum(parts_ref[...].astype(jnp.float32), axis=0)


def to_all(own, axes):
    copies = jnp.broadcast_to(own[None], (lax.axis_size(axes), *own.shape))
    return lax.all_to_all(copies, axes, 0, 0)


def gather_pairs(partial, diag, pairs):
    diag = jnp.pad(diag, ((0, 0), (0, 8 - diag.shape[1]), (0, 0)))
    return lax.all_gather(jnp.concatenate([partial, diag], axis=0), "zh", axis_index_groups=pairs)


def vectors_of(blocks):
    return blocks.transpose(1, 0, 2).reshape(blocks.shape[1], -1)


def body(x_cols, diag_rows, theta, tiles, tile_rows, tile_cols, counts):
    core = lax.axis_index("c")
    slots, width = tiles.shape[2], tiles.shape[3]
    rows = jnp.pad(tile_rows[0, 0], (0, 32))
    cols = jnp.pad(tile_cols[0, 0], (0, 32))
    slot = jnp.arange(slots + 32, dtype=jnp.int32)
    used = slot < counts[0, 0]
    table = jnp.where(used, ((place(rows >> 2, core) << 2) | (rows & 3)) << 8 | cols, 128 << 8 | 64)
    table = jnp.where(slot == AT_ROW, lax.axis_index(ROW), table)
    table = jnp.where(slot == AT_COL, lax.axis_index(COL), table)
    table = jnp.where(slot == AT_CORE, core, table)
    table = jnp.where(slot == AT_ZH, lax.axis_index("zh"), table).astype(jnp.float32)
    table = jnp.where(slot < AT_THETA, table, jnp.pad(theta, (AT_THETA, 16)))

    smem = pl.BlockSpec(memory_space=pltpu.SMEM)
    vmem = pl.BlockSpec(memory_space=pltpu.VMEM)
    params = pltpu.CompilerParams(vmem_limit_bytes=16 * 1024 * 1024)
    cost = pl.CostEstimate(flops=2 * slots * 8 * width * width, bytes_accessed=4 << 20, transcendentals=0)
    f32 = functools.partial(jax.ShapeDtypeStruct, dtype=jnp.float32)

    tiles_here = tiles.reshape(slots // 2, 2 * width, width)
    table = pl.pallas_call(
        settle,
        out_shape=f32(table.shape),
        in_specs=[vmem],
        out_specs=vmem,
        compiler_params=params,
        cost_estimate=pl.CostEstimate(flops=1 << 31, bytes_accessed=8 << 20, transcendentals=0),
    )(table)

    own = x_cols.reshape(8, 4, width).transpose(1, 0, 2)
    x_all = to_all(own, ROW).reshape(64, 8, width)
    partial = pl.pallas_call(
        forward,
        out_shape=f32((128, 8, width)),
        in_specs=[vmem, vmem, vmem],
        out_specs=vmem,
        scratch_shapes=[pltpu.VMEM((136, 8, width), jnp.float32), pltpu.SMEM((128,), jnp.float32), pltpu.SemaphoreType.DMA],
        compiler_params=params,
        cost_estimate=cost,
    )(table, tiles_here, x_all)

    partial = partial.reshape(4, 2, 16, 8, width)
    halves = lax.all_gather(partial[:, 1], "c")
    partial = partial[:, 0] + lax.dynamic_index_in_dim(halves, 1 - core, 0, keepdims=False)
    partial = jnp.sum(lax.all_to_all(partial, "y", 0, 0), axis=0)
    got = gather_pairs(partial, diag_rows.reshape(1, 4, width), [[0, 3], [1, 2]])
    diag = got[:, 16, :4].reshape(1, 8, width)
    got = gather_pairs(got[0, :16] + got[1, :16], diag, [[0, 1], [3, 2]])
    resid = got[0, :16] + got[1, :16]
    diag = got[:, 16]
    diag = jnp.concatenate([diag[0, :4], diag[1], diag[0, 4:]], axis=0).reshape(16, 1, width)
    scaled = to_all((resid / diag).astype(jnp.bfloat16), ("y", "c")).reshape(128, 8, width)

    back, resid = pl.pallas_call(
        backward,
        out_shape=(jax.ShapeDtypeStruct((64, 8, width), BACK), pltpu.VMEM((4, 8, width), jnp.float32)),
        in_specs=[vmem, vmem, vmem, vmem],
        out_specs=(vmem, vmem),
        scratch_shapes=[pltpu.VMEM((72, 8, width), jnp.float32), pltpu.SMEM((128,), jnp.float32), pltpu.SemaphoreType.DMA],
        compiler_params=params,
        cost_estimate=cost,
    )(table, tiles_here, scaled, resid)
    image, resid = pl.pallas_call(
        finish,
        out_shape=(f32((4, 8, width)), f32((4, 8, width))),
        in_specs=[vmem, vmem],
        out_specs=(vmem, vmem),
        compiler_params=params,
    )(lax.all_to_all(back.reshape(16, 4, 8, width), ROW, 0, 0), resid)
    return vectors_of(resid), vectors_of(image)


def solution(mesh):
    fine = Mesh(mesh.devices.reshape(4, 4, 4, 4, 2), ROW + COL)
    return jax.shard_map(
        body,
        mesh=fine,
        in_specs=(
            P(None, COL + ROW),
            P(ROW + COL),
            P(),
            P(ROW, COL, None, None, None),
            P(ROW, COL, None),
            P(ROW, COL, None),
            P(ROW, COL),
        ),
        out_specs=(P(None, ROW + COL), P(None, COL + ROW)),
        check_vma=False,
    )
```
